32 devices in a mesh: rep: 2 (over x), mp: 16 (over z, y, core).
Axes of the slice: x: 2, y: 2, z: 4, core: 2. Of those that a mesh axis runs over, the one named last changes fastest.
Arguments:
- tokens: bfloat16 [2, 1024, 5120], P('rep', 'mp'), may hold values from -6 to 6
- prompt_ids: int32 [2, 1024], P('rep', 'mp'), may hold values from 0 to 11, never falling along the last dimension, each value on 1 to 256 neighbouring positions
- modulation: float32 [2, 12, 3, 5120], P('rep'), may hold values from -4 to 4
- trainer_up: float32 [5120, 13824], P('mp', 'rep'), may hold values from -0.078125 to 0.078125
- trainer_down: float32 [13824, 5120], P('rep', 'mp'), may hold values from -0.0546875 to 0.0546875
Outputs:
- result: bfloat16 [2, 1024, 5120], P('rep', 'mp')
The draws below stay inside these ranges and needn't reach their ends.
Inputs may be any that keep to these rules, and one draw needn't show every extreme that they name: `prompt_ids`: along each replica's 1024 tokens the prompt number never falls; each of the 12 prompts has at least one token, and one prompt has exactly a quarter of 1024.
All inputs are finite; a program needn't handle non-finite values.
Results may differ from the reference program's by a relative error of at most 0.023.
Values may be sent and summed in bfloat16 or wider, within the bound.
No kernel may reach another device: no remote copies, remote signals or barrier semaphores. Data moves between devices by JAX's collectives and lax.ppermute only.
A program may use at most 192 MiB of HBM per device.

```python
import math
import jax
import jax.numpy as jnp
import numpy as np
from jax import lax

D = 5120
FF = 13824
PROMPTS_REP = 12
T_REP = 1024
N_REP = 2
N_MP = 16


def draw_tokens(key, part):
    key_offset, key_spread, key_base = jax.random.split(key, 3)
    offset = jax.random.uniform(key_offset, (N_REP, T_REP, 1), jnp.float32, -2.0, 2.0)
    spread = jnp.exp(jax.random.uniform(key_spread, (N_REP, T_REP, 1), jnp.float32, math.log(0.35), math.log(1.3)))
    base = jnp.clip(jax.random.normal(key_base, (N_REP, T_REP, D), jnp.float32), -3.0, 3.0)
    values = offset + spread * base
    return values.astype(jnp.bfloat16)


def levels(key, extent, cuts, smallest, high):
    def one(axis_at, blocks):
        draws = jax.random.uniform(jax.random.fold_in(jax.random.fold_in(key, 6), axis_at), (blocks,), jnp.float32, smallest / len(cuts), high / len(cuts))
        return jnp.repeat(jnp.exp(draws), extent[axis_at] // blocks).reshape((-1,) + (1,) * (len(extent) - axis_at - 1))

    loudness = one(*cuts[0])
    for cut in cuts[1:]:
        loudness = loudness * one(*cut)
    return loudness


def split_up(number_of, total, most, slope):
    portions = [(1 << 20) // math.isqrt(rank ** slope) + 1 for rank in range(2, number_of + 1)]
    rest, counts = total - most - (number_of - 1), [1] * (number_of - 1)
    while rest > 0:
        candidates = [i for i in range(number_of - 1) if counts[i] < most]
        mass, left = sum([portions[i] for i in candidates]), rest
        for i in candidates:
            addition = min(most - counts[i], max(1, left * portions[i] // mass), rest)
            counts[i] = counts[i] + addition
            rest = rest - addition
    return np.array([most] + counts)


def uneven(own_key, amount, total, limit, skew):
    if amount == 2:
        one = jax.random.randint(own_key, (), max(1, total - limit), min(limit, total - 1) + 1)
        return jnp.stack([one, total - one])
    lengths = jnp.asarray(split_up(amount, total, limit, skew), jnp.int32)
    twos = (amount - 1) // 2
    source_of, sink = lengths[1:1 + 2 * twos:2], lengths[2:2 + 2 * twos:2]
    room = jnp.minimum(source_of - 1, limit - sink)
    passed = jax.random.randint(jax.random.fold_in(own_key, 1), (twos,), 0, 1 << 20) % (room + 1)
    lengths = lengths.at[1:1 + 2 * twos:2].set(source_of - passed).at[2:2 + 2 * twos:2].set(sink + passed)
    return lengths[jax.random.permutation(jax.random.fold_in(own_key, 2), amount)]


def scatter_about(rng, extent, deviation, reach, cuts=(), kind=jnp.bfloat16):
    values = jax.random.normal(rng, extent, jnp.float32) * deviation
    if len(cuts) > 0:
        values = levels(rng, extent, cuts, -0.22, 0.18) * values
    return jnp.clip(values, min=-reach, max=reach).astype(kind)


def setup_inputs(seed: int = 0) -> dict:
    seeds = jax.random.split(jax.random.key(seed), 6)
    return {
        "tokens": draw_tokens(jax.random.fold_in(seeds[5], 71), 0),
        "prompt_ids": jax.vmap(lambda own: jnp.searchsorted(jnp.cumsum(uneven(own, PROMPTS_REP, T_REP, T_REP // 4, 2)), jnp.arange(T_REP), side="right"))(jax.random.split(seeds[1], N_REP)).reshape((N_REP, T_REP)).astype(jnp.int32),
        "modulation": scatter_about(seeds[2], (N_REP, PROMPTS_REP, 3, D), 0.7, 4.0, ((0, 2),), jnp.float32),
        "trainer_up": scatter_about(seeds[3], (D, FF), D ** -0.5, 0.078125, ((0, 16), (1, 2)), jnp.float32),
        "trainer_down": scatter_about(seeds[4], (FF, D), FF ** -0.5, 0.0546875, ((0, 2), (1, 16)), jnp.float32),
    }


def reference(tokens, prompt_ids, modulation, trainer_up, trainer_down):
    as_float = tokens.astype(jnp.float32)
    average = lax.optimization_barrier(jnp.mean(as_float, axis=-1, keepdims=True))
    centred = as_float - average
    variance = lax.optimization_barrier(jnp.mean(centred * centred, axis=-1, keepdims=True))
    normed = centred / jnp.sqrt(variance + 1e-06)
    onehot = (prompt_ids[:, :, None] == jnp.arange(PROMPTS_REP, dtype=jnp.int32)[None, None, :]).astype(jnp.float32)
    chosen = jnp.einsum('rtp,rpkd->rtkd', onehot, modulation, precision=lax.Precision.HIGHEST)
    shift = chosen[:, :, 0]
    scale = chosen[:, :, 1]
    gate = chosen[:, :, 2]
    xin = (normed * (1.0 + scale) + shift).astype(jnp.bfloat16)
    w_up = trainer_up.astype(jnp.bfloat16)
    w_down = trainer_down.astype(jnp.bfloat16)
    flat = xin.reshape(N_REP * T_REP, D)
    hidden = jax.nn.gelu(jnp.dot(flat, w_up, preferred_element_type=jnp.float32), approximate=True).astype(jnp.bfloat16)
    group = FF // N_MP
    hid_groups = hidden.reshape(N_REP * T_REP, N_MP, group).transpose(1, 0, 2)
    down_groups = w_down.reshape(N_MP, group, D)

    def add_group(index, total):
        partial_sum = jnp.dot(hid_groups[index], down_groups[index], preferred_element_type=jnp.float32).astype(jnp.bfloat16)
        partial_sum = lax.optimization_barrier(partial_sum)
        return total + partial_sum.astype(jnp.float32)
    mlp = lax.fori_loop(0, N_MP, add_group, jnp.zeros((N_REP * T_REP, D), jnp.float32))
    result = as_float + gate * mlp.reshape(N_REP, T_REP, D)
    return result.astype(jnp.bfloat16)
```

```python
import jax
import jax.numpy as jnp
from jax import lax
from jax.sharding import PartitionSpec as P

BF = jnp.bfloat16
F32 = jnp.float32


def modulated(tokens, prompt_ids, modulation):
    as_float = tokens[0].astype(F32)
    average = jnp.mean(as_float, axis=-1, keepdims=True)
    centred = as_float - average
    variance = jnp.mean(centred * centred, axis=-1, keepdims=True)
    normed = centred / jnp.sqrt(variance + 1e-06)
    prompts_here = modulation.shape[1]
    onehot = (prompt_ids[0][:, None] == jnp.arange(prompts_here, dtype=jnp.int32)[None, :]).astype(F32)
    chosen = jnp.einsum("tp,pkd->tkd", onehot, modulation[0], precision=lax.Precision.HIGHEST)
    shift = chosen[:, 0]
    scale = chosen[:, 1]
    gate = chosen[:, 2]
    xin = (normed * (1.0 + scale) + shift).astype(BF)
    return as_float, gate, xin


def gathered_weights(tokens, prompt_ids, modulation, trainer_up, trainer_down):
    as_float, gate, xin = modulated(tokens, prompt_ids, modulation)
    up_rows = lax.all_gather(trainer_up.astype(BF), "rep", axis=1, tiled=True)
    w_up = lax.all_to_all(up_rows, "mp", split_axis=1, concat_axis=0, tiled=True)
    down_columns = lax.all_gather(trainer_down.astype(BF), "rep", axis=0, tiled=True)
    w_down = lax.all_to_all(down_columns, "mp", split_axis=0, concat_axis=1, tiled=True)
    everyone = lax.all_gather(xin, "mp", axis=0, tiled=True)
    hidden = jax.nn.gelu(jnp.dot(everyone, w_up, preferred_element_type=F32), approximate=True).astype(BF)
    partial = jnp.dot(hidden, w_down, preferred_element_type=F32).astype(BF)
    mlp = lax.psum_scatter(partial, "mp", scatter_dimension=0, tiled=True).astype(F32)
    return (as_float + gate * mlp).astype(BF)[None]


def xor_mp(value, mask):
    return lax.ppermute(value, "mp", [(i, i ^ mask) for i in range(16)])


def swap_rep(value):
    return lax.ppermute(value, "rep", [(0, 1), (1, 0)])


def in_order(received, index):
    low = (index & 1) == 1
    high = (index & 2) == 2
    a, b, c, d = received
    a, b = jnp.where(low, b, a), jnp.where(low, a, b)
    c, d = jnp.where(low, d, c), jnp.where(low, c, d)
    return [jnp.where(high, c, a), jnp.where(high, d, b), jnp.where(high, a, c), jnp.where(high, b, d)]


def tie(first, second):
    return lax.optimization_barrier((first, second))


ORDER = ((0, 0), (1, 0), (2, 0), (3, 0), (3, 1), (2, 1), (1, 1), (3, 2), (2, 2), (3, 3), (2, 3), (0, 1), (1, 2), (1, 3), (0, 2), (0, 3))


def planes(tokens, prompt_ids, modulation, trainer_up, trainer_down):
    me = lax.axis_index("mp")
    z, j = me // 4, me % 4
    y, c = j // 2, j % 2
    is_mid = (z == 1) | (z == 2)
    rows = trainer_up.shape[0]
    units = trainer_up.shape[1] // 4
    wide = units * 8 // 27 // 128 * 128
    widths = [wide, wide, wide, units - 3 * wide]
    starts = [4 * sum(widths[:k]) for k in range(4)]
    sources = {"up": trainer_up, "down": trainer_down.T}
    weight = {}

    def cut(matrix, k, at):
        return lax.dynamic_slice(matrix, (0, starts[k] + at * 2 * widths[k]), (rows, 2 * widths[k])).astype(BF)

    def y_phase(items, token=None):
        sent, kept = [], []
        for name, k in items:
            matrix = sources[name]
            if token is not None:
                matrix, token = tie(matrix, token)
            sent.append(cut(matrix, k, 1 - y))
            kept.append(cut(matrix, k, y))
        got = xor_mp(jnp.concatenate(sent, axis=0), 2)
        return (items, kept, got), token

    def c_phase(state, token=None):
        items, kept, got = state
        if token is not None:
            got, token = tie(got, token)
        width = widths[items[0][1]]
        both = jnp.concatenate(kept + [got], axis=0)
        keep = lax.dynamic_slice(both, (0, c * width), (both.shape[0], width))
        give = lax.dynamic_slice(both, (0, (1 - c) * width), (both.shape[0], width))
        came = xor_mp(give, 1)
        n = len(items)
        for i, item in enumerate(items):
            mine, theirs = slice(i * rows, (i + 1) * rows), slice((n + i) * rows, (n + i + 1) * rows)
            weight[item] = jnp.concatenate(in_order([keep[mine], came[mine], keep[theirs], came[theirs]], j), axis=0)
        return token

    first, _ = y_phase([("up", 0)])
    as_float, gate, xin = modulated(tokens, prompt_ids, modulation)
    owned = xin.shape[0]
    part = xin.shape[1] // 4

    def cut_in(m):
        return lax.dynamic_slice(xin, (0, (z ^ m) * part), (owned, part))

    received = [cut_in(0)] + [xor_mp(cut_in(m), 4 * m) for m in (1, 2, 3)]
    here = jnp.concatenate(in_order(received, z), axis=0)
    c_phase(first)
    beside = xor_mp(here, 2)
    there = swap_rep(here)
    far = swap_rep(beside)
    xs = [jnp.concatenate([block, xor_mp(block, 1)], axis=0) for block in (here, beside, there, far)]

    to_other = [(i, i ^ 12) for i in range(16) if i // 4 in (1, 2)]
    outs = [None] * 4
    sums = [None] * 4
    waiting = {}
    jobs = {
        0: [("y", (("up", 1),)), ("y", (("down", 0),))],
        1: [("c", (("up", 1),)), ("y", (("down", 1),))],
        2: [("c", (("down", 0),)), ("y", (("up", 2), ("down", 2)))],
        3: [("c", (("down", 1),)), ("y", (("up", 3), ("down", 3)))],
        5: [("c", (("up", 2), ("down", 2)))],
        6: [("c", (("up", 3), ("down", 3)))],
    }
    left = [4] * 4
    count = len(ORDER)
    mine, arrived, total, other, done = {}, {}, {}, {}, {}
    for s in range(count + 4):
        if s < count:
            block, k = ORDER[s]
            mine[s] = lax.dot_general(weight["up", k], xs[block], (((0,), (1,)), ((), ())), preferred_element_type=F32)
        if s < count + 3:
            outgoing = []
            if s < count:
                outgoing.append(mine[s].astype(BF))
            if s >= 3:
                outgoing.append(done[s - 3])
            if len(outgoing) == 2:
                p, h = outgoing
                tall = max(p.shape[0], h.shape[0])
                p, h = [jnp.pad(v, ((0, tall - v.shape[0]), (0, 0))) for v in (p, h)]
                payload = jnp.where(is_mid, h, p)
            else:
                payload = outgoing[0]
            arrived[s] = xor_mp(payload, 4)
        if s < count:
            for kind, items in jobs.get(s, []):
                if kind == "y":
                    waiting[items], mine[s] = y_phase(items, mine[s])
                else:
                    mine[s] = c_phase(waiting.pop(items), mine[s])
            if s >= 1:
                arrived[s - 1], mine[s] = tie(arrived[s - 1], mine[s])
        if 0 <= s - 1 < count:
            total[s - 1] = mine[s - 1] + arrived[s - 1][: mine[s - 1].shape[0]].astype(F32)
            other[s - 1] = lax.ppermute(total[s - 1].astype(BF), "mp", to_other)
            if s >= 2:
                other[s - 2], total[s - 1] = tie(other[s - 2], total[s - 1])
        if 0 <= s - 2 < count:
            done[s - 2] = jax.nn.gelu(total[s - 2] + other[s - 2].astype(F32), approximate=True).astype(BF)
        if 0 <= s - 4 < count:
            block, k = ORDER[s - 4]
            hidden = done[s - 4]
            hidden = jnp.where(is_mid, hidden, arrived[s - 1][: hidden.shape[0]])
            term = lax.dot_general(hidden, weight["down", k], (((0,), (1,)), ((), ())), preferred_element_type=F32)
            outs[block] = term if outs[block] is None else outs[block] + term
            left[block] -= 1
            if left[block] == 0:
                size = owned * 4
                sums[block] = outs[block][:size] + xor_mp(outs[block][size:].astype(BF), 1).astype(F32)
            elif s + 1 < count:
                outs[block], xs[ORDER[s + 1][0]] = tie(outs[block], xs[ORDER[s + 1][0]])

    side = sums[1] + swap_rep(sums[3].astype(BF)).astype(F32)
    summed = sums[0] + swap_rep(sums[2].astype(BF)).astype(F32)
    summed = (summed + xor_mp(side.astype(BF), 2).astype(F32)).astype(BF)

    def cut_out(m):
        return lax.dynamic_slice(summed, ((z ^ m) * owned, 0), (owned, part))

    received = [cut_out(0)] + [xor_mp(cut_out(m), 4 * m) for m in (1, 2, 3)]
    mlp = jnp.concatenate(in_order(received, z), axis=1).astype(F32)
    return (as_float + gate * mlp).astype(BF)[None]


def solution(mesh):
    in_specs = (
        P("rep", "mp", None),
        P("rep", "mp"),
        P("rep", None, None, None),
        P("mp", "rep"),
        P("rep", "mp"),
    )
    out_specs = P("rep", "mp", None)
    local = planes if (mesh.shape["rep"], mesh.shape["mp"]) == (2, 16) else gathered_weights
    return jax.shard_map(local, mesh=mesh, in_specs=in_specs, out_specs=out_specs, check_vma=False)
```

```python
import jax
import jax.numpy as jnp
from jax import lax
from jax.experimental import pallas as pl
from jax.experimental.pallas import tpu as pltpu
from jax.sharding import PartitionSpec as P

BF = jnp.bfloat16
F32 = jnp.float32


def chosen(prompt_ids, vectors):
    prompts_here = vectors.shape[0]
    onehot = (prompt_ids[0][:, None] == jnp.arange(prompts_here, dtype=jnp.int32)[None, :]).astype(F32)
    return jnp.einsum("tp,pkd->tkd", onehot, vectors, precision=lax.Precision.HIGHEST)


def modulated(tokens, prompt_ids, modulation):
    as_float = tokens[0].astype(F32)
    average = jnp.mean(as_float, axis=-1, keepdims=True)
    centred = as_float - average
    variance = jnp.mean(centred * centred, axis=-1, keepdims=True)
    normed = centred / jnp.sqrt(variance + 1e-06)
    vectors = chosen(prompt_ids, modulation[0, :, :2])
    return (normed * (1.0 + vectors[:, 1]) + vectors[:, 0]).astype(BF)


def gathered_weights(tokens, prompt_ids, modulation, trainer_up, trainer_down):
    xin = modulated(tokens, prompt_ids, modulation)
    gate = chosen(prompt_ids, modulation[0, :, 2:])[:, 0]
    up_rows = lax.all_gather(trainer_up.astype(BF), "rep", axis=1, tiled=True)
    w_up = lax.all_to_all(up_rows, "mp", split_axis=1, concat_axis=0, tiled=True)
    down_columns = lax.all_gather(trainer_down.astype(BF), "rep", axis=0, tiled=True)
    w_down = lax.all_to_all(down_columns, "mp", split_axis=0, concat_axis=1, tiled=True)
    everyone = lax.all_gather(xin, "mp", axis=0, tiled=True)
    hidden = jax.nn.gelu(jnp.dot(everyone, w_up, preferred_element_type=F32), approximate=True).astype(BF)
    partial = jnp.dot(hidden, w_down, preferred_element_type=F32).astype(BF)
    mlp = lax.psum_scatter(partial, "mp", scatter_dimension=0, tiled=True).astype(F32)
    return (tokens[0].astype(F32) + gate * mlp).astype(BF)[None]


def xor_mp(value, mask):
    return lax.ppermute(value, "mp", [(i, i ^ mask) for i in range(16)])


def swap_rep(value):
    return lax.ppermute(value, "rep", [(0, 1), (1, 0)])


def in_order(received, index):
    low = (index & 1) == 1
    high = (index & 2) == 2
    a, b, c, d = received
    a, b = jnp.where(low, b, a), jnp.where(low, a, b)
    c, d = jnp.where(low, d, c), jnp.where(low, c, d)
    return [jnp.where(high, c, a), jnp.where(high, d, b), jnp.where(high, a, c), jnp.where(high, b, d)]


def tie(first, second):
    return lax.optimization_barrier((first, second))


ORDER = ((0, 0), (1, 0), (2, 0), (3, 0), (3, 1), (1, 1), (2, 1), (0, 1), (3, 2), (1, 2), (3, 3), (1, 3), (2, 2), (2, 3), (0, 2), (0, 3))


def prepared(matrix, widths, groups):
    rows, columns = matrix.shape
    starts = [4 * sum(widths[:k]) for k in range(len(widths))]
    outs = [sum(widths[k] for k in group) for group in groups]
    width = widths[0]
    single = groups == [[0]] and width % 128 == 0
    if single:
        step = rows // 2 if rows % 32 == 0 else rows
        specs = [pl.BlockSpec((step, width), lambda r, d=d: (r, d)) for d in range(4)]
    else:
        step = 64 if rows % 64 == 0 else 32
        specs = [pl.BlockSpec((step, columns // 2), lambda r, d=d: (r, d)) for d in range(2)]

    def copy(sources, target, at, begin, size):
        for part in range(2):
            base = part * columns // 2
            low, high = max(begin, base), min(begin + size, base + columns // 2)
            if low < high:
                target[:, at + low - begin : at + high - begin] = sources[part][:, low - base : high - base].astype(BF)

    def kernel(*refs):
        sources, targets = refs[: len(specs)], refs[len(specs) :]
        for target, group in zip(targets, groups, strict=True):
            for d in range(4):
                if single:
                    target[d] = sources[d][...].astype(BF)
                    continue
                at = 0
                for k in group:
                    copy(sources, target.at[d], at, starts[k] + d * widths[k], widths[k])
                    at += widths[k]

    return pl.pallas_call(
        kernel,
        grid=(rows // step,),
        in_specs=specs,
        out_specs=[pl.BlockSpec((4, step, w), lambda r: (0, r, 0)) for w in outs],
        out_shape=[jax.ShapeDtypeStruct((4, rows, w), BF) for w in outs],
        compiler_params=pltpu.CompilerParams(vmem_limit_bytes=56 * 2**20),
        cost_estimate=pl.CostEstimate(flops=0, bytes_accessed=24 * rows * sum(outs), transcendentals=0),
    )(*[matrix] * len(specs))


def up_product(halves, matrix, start, width):
    count, features = halves[0].shape

    def kernel(first, second, matrix_ref, out):
        weights = matrix_ref[:, :, start : start + width].reshape(features, width)
        out[:count] = jnp.dot(first[...], weights, preferred_element_type=F32).astype(BF)
        out[count:] = jnp.dot(second[...], weights, preferred_element_type=F32).astype(BF)

    return pl.pallas_call(
        kernel,
        out_shape=jax.ShapeDtypeStruct((2 * count, width), BF),
        compiler_params=pltpu.CompilerParams(vmem_limit_bytes=16 * 2**20),
        cost_estimate=pl.CostEstimate(flops=4 * count * features * width, bytes_accessed=2 * (2 * count + width) * features + 4 * count * width, transcendentals=0),
    )(*halves, matrix)


def down_product(flag, pairs, matrix, places, before, split):
    n = len(pairs)
    features = matrix.shape[0] * matrix.shape[1]
    count = pairs[0][0].shape[0]
    half = count // 2

    def kernel(flag_ref, *refs):
        made, sent = refs[:n], refs[n : 2 * n]
        matrix_ref, rest = refs[2 * n], refs[2 * n + 1 :]
        step = pl.program_id(0)
        at = pl.ds(pl.multiple_of((1 - step) * half, half), half)
        total = rest[0][at, :] if before is not None else None
        for i, (start, width) in enumerate(places):
            hidden = jnp.where(flag_ref[0] == 1, made[i][at, :], sent[i][at, :width])
            weights = matrix_ref[:, :, start : start + width].reshape(features, width)
            term = lax.dot_general(hidden, weights, (((1,), (1,)), ((), ())), preferred_element_type=F32)
            total = term if total is None else total + term
        if not split:
            rest[-1][at, :] = total
            return

        @pl.when(step == 0)
        def _():
            rest[-1][...] = total.astype(BF)

        @pl.when(step == 1)
        def _():
            rest[-2][...] = total

    operands = [m for m, _ in pairs] + [t for _, t in pairs] + [matrix]
    if before is not None:
        operands.append(before)
    specs = [pl.BlockSpec(m.shape, lambda r, n=len(m.shape): (0,) * n) for m in operands]
    if split:
        shapes = [jax.ShapeDtypeStruct((half, features), F32), jax.ShapeDtypeStruct((half, features), BF)]
    else:
        shapes = [jax.ShapeDtypeStruct((count, features), F32)]
    depth = sum(w for _, w in places)
    return pl.pallas_call(
        kernel,
        grid=(2,),
        in_specs=[pl.BlockSpec(memory_space=pltpu.SMEM)] + specs,
        out_specs=[pl.BlockSpec(o.shape, lambda r: (0, 0)) for o in shapes],
        out_shape=shapes,
        compiler_params=pltpu.CompilerParams(vmem_limit_bytes=32 * 2**20),
        cost_estimate=pl.CostEstimate(flops=2 * depth * features * count, bytes_accessed=2 * depth * (features + 2 * count) + 4 * features * count, transcendentals=0),
    )(flag, *operands)


def planes(tokens, prompt_ids, modulation, trainer_up, trainer_down):
    me = lax.axis_index("mp")
    z = me // 4
    is_mid = (z == 1) | (z == 2)
    flag = is_mid.astype(jnp.int32).reshape(1)
    rows = trainer_up.shape[0]
    units = trainer_up.shape[1] // 4
    wide = units * 8 // 27 // 128 * 128
    widths = [wide, wide, wide, units - 3 * wide]
    down_t = trainer_down.T
    groups = [list(range(4 * p, 4 * p + 4)) for p in range(4)]

    def spread(sent, token=None):
        if token is not None:
            sent, token = tie(sent, token)
        return lax.all_to_all(sent, "mp", 0, 0, axis_index_groups=groups, tiled=True), token

    (up_first,) = prepared(trainer_up, widths, [[0]])
    up = [spread(up_first)[0]]
    xin = modulated(tokens, prompt_ids, modulation)
    owned = xin.shape[0]
    part = xin.shape[1] // 4

    def cut_in(m):
        return lax.dynamic_slice(xin, (0, (z ^ m) * part), (owned, part))

    received = [cut_in(0)] + [xor_mp(cut_in(m), 4 * m) for m in (1, 2, 3)]
    here = jnp.concatenate(in_order(received, z), axis=0)
    ready = list(prepared(trainer_up, widths, [[1], [2, 3]]))
    up[0], here = tie(up[0], here)
    ready[0], here = tie(ready[0], here)
    beside = xor_mp(here, 2)
    there = swap_rep(here)
    xs = [(here, xor_mp(here, 1)), None, None, None]

    to_other = [(i, i ^ 12) for i in range(16) if i // 4 in (1, 2)]
    early = [0, 0, 0, widths[2]]
    late = [sum(widths[:k]) for k in range(4)]
    outs = [None] * 4
    sums = [None] * 4
    left = [4] * 4
    held = [[] for _ in range(4)]
    pending = None
    count = len(ORDER)
    mine, arrived, total, other, done = {}, {}, {}, {}, {}
    for s in range(count + 4):
        if s < count:
            block, k = ORDER[s]
            if s == 1:
                down_t, mine[0] = tie(down_t, mine[0])
                (ready_down,) = prepared(down_t, widths, [[0, 1, 2, 3]])
                beside, ready_down = tie(beside, ready_down)
                there, mine[0] = tie(there, mine[0])
                far = swap_rep(beside)
                for i, value in ((1, beside), (2, there), (3, far)):
                    xs[i] = (value, xor_mp(value, 1))
            first, second = xs[block]
            if s >= 2:
                first, total[s - 2] = tie(first, total[s - 2])
            if s == 3:
                first, up[1] = tie(first, up[1])
            if s == 6:
                first, up[2] = tie(first, up[2])
            if pending is not None:
                first, outs[pending] = tie(first, outs[pending])
                pending = None
            mine[s] = up_product((first, second), up[min(k, 2)], early[k], widths[k])
        if s < count + 3:
            outgoing = []
            if s < count:
                outgoing.append(mine[s])
            if s >= 3:
                outgoing.append(done[s - 3])
            if len(outgoing) == 2:
                p, h = outgoing
                broad = max(p.shape[1], h.shape[1])
                p, h = [jnp.pad(v, ((0, 0), (0, broad - v.shape[1]))) for v in (p, h)]
                payload = jnp.where(is_mid, h, p)
            else:
                payload = outgoing[0]
            arrived[s] = xor_mp(payload, 4)
        if s < count:
            if s < 2:
                got, mine[s] = spread(ready[s], mine[s])
                up.append(got)
            if s == 2:
                down, mine[s] = spread(ready_down, mine[s])
            if s >= 1:
                arrived[s - 1], mine[s] = tie(arrived[s - 1], mine[s])
        if 0 <= s - 1 < count:
            term = arrived[s - 1][:, : mine[s - 1].shape[1]]
            total[s - 1] = (mine[s - 1].astype(F32) + term.astype(F32)).astype(BF)
            other[s - 1] = lax.ppermute(total[s - 1], "mp", to_other)
            if s >= 2:
                other[s - 2], total[s - 1] = tie(other[s - 2], total[s - 1])
        if 0 <= s - 2 < count:
            summed = total[s - 2].astype(F32) + other[s - 2].astype(F32)
            done[s - 2] = jax.nn.gelu(summed, approximate=True).astype(BF)
        if 0 <= s - 4 < count:
            block, k = ORDER[s - 4]
            held[block].append((done[s - 4], arrived[s - 1], k))
            left[block] -= 1
            if len(held[block]) == 2:
                pairs = [(d, t) for d, t, _ in held[block]]
                places = [(late[i], widths[i]) for _, _, i in held[block]]
                held[block] = []
                made = down_product(flag, pairs, down, places, outs[block], left[block] == 0)
                if left[block] == 0:
                    sums[block] = made[0] + xor_mp(made[1], 1).astype(F32)
                else:
                    (outs[block],) = made
                    pending = block

    side = sums[1] + swap_rep(sums[3].astype(BF)).astype(F32)
    summed = sums[0] + swap_rep(sums[2].astype(BF)).astype(F32)
    summed = (summed + xor_mp(side.astype(BF), 2).astype(F32)).astype(BF)

    def cut_out(m):
        return lax.dynamic_slice(summed, ((z ^ m) * owned, 0), (owned, part))

    received = [cut_out(0)] + [xor_mp(cut_out(m), 4 * m) for m in (1, 2, 3)]
    mlp = jnp.concatenate(in_order(received, z), axis=1).astype(F32)
    prompt_ids, _ = tie(prompt_ids, mine[count - 1])
    gate = chosen(prompt_ids, modulation[0, :, 2:])[:, 0]
    return (tokens[0].astype(F32) + gate * mlp).astype(BF)[None]


def solution(mesh):
    in_specs = (
        P("rep", "mp", None),
        P("rep", "mp"),
        P("rep", None, None, None),
        P("mp", "rep"),
        P("rep", "mp"),
    )
    out_specs = P("rep", "mp", None)
    local = planes if (mesh.shape["rep"], mesh.shape["mp"]) == (2, 16) else gathered_weights
    return jax.shard_map(local, mesh=mesh, in_specs=in_specs, out_specs=out_specs, check_vma=False)
```

```python
import jax
import jax.numpy as jnp
from jax import lax
from jax.experimental import pallas as pl
from jax.experimental.pallas import tpu as pltpu
from jax.sharding import PartitionSpec as P

BF = jnp.bfloat16
F32 = jnp.float32


def chosen(prompt_ids, vectors):
    prompts_here = vectors.shape[0]
    onehot = (prompt_ids[0][:, None] == jnp.arange(prompts_here, dtype=jnp.int32)[None, :]).astype(F32)
    return jnp.einsum("tp,pkd->tkd", onehot, vectors, precision=lax.Precision.HIGHEST)


def modulated(tokens, prompt_ids, modulation):
    as_float = tokens[0].astype(F32)
    average = jnp.mean(as_float, axis=-1, keepdims=True)
    centred = as_float - average
    variance = jnp.mean(centred * centred, axis=-1, keepdims=True)
    normed = centred / jnp.sqrt(variance + 1e-06)
    vectors = chosen(prompt_ids, modulation[0, :, :2])
    return (normed * (1.0 + vectors[:, 1]) + vectors[:, 0]).astype(BF)


def gathered_weights(tokens, prompt_ids, modulation, trainer_up, trainer_down):
    xin = modulated(tokens, prompt_ids, modulation)
    gate = chosen(prompt_ids, modulation[0, :, 2:])[:, 0]
    up_rows = lax.all_gather(trainer_up.astype(BF), "rep", axis=1, tiled=True)
    w_up = lax.all_to_all(up_rows, "mp", split_axis=1, concat_axis=0, tiled=True)
    down_columns = lax.all_gather(trainer_down.astype(BF), "rep", axis=0, tiled=True)
    w_down = lax.all_to_all(down_columns, "mp", split_axis=0, concat_axis=1, tiled=True)
    everyone = lax.all_gather(xin, "mp", axis=0, tiled=True)
    hidden = jax.nn.gelu(jnp.dot(everyone, w_up, preferred_element_type=F32), approximate=True).astype(BF)
    partial = jnp.dot(hidden, w_down, preferred_element_type=F32).astype(BF)
    mlp = lax.psum_scatter(partial, "mp", scatter_dimension=0, tiled=True).astype(F32)
    return (tokens[0].astype(F32) + gate * mlp).astype(BF)[None]


def xor_mp(value, mask):
    return lax.ppermute(value, "mp", [(i, i ^ mask) for i in range(16)])


def swap_rep(value):
    return lax.ppermute(value, "rep", [(0, 1), (1, 0)])


def in_order(received, index):
    low = (index & 1) == 1
    high = (index & 2) == 2
    a, b, c, d = received
    a, b = jnp.where(low, b, a), jnp.where(low, a, b)
    c, d = jnp.where(low, d, c), jnp.where(low, c, d)
    return [jnp.where(high, c, a), jnp.where(high, d, b), jnp.where(high, a, c), jnp.where(high, b, d)]


def tie(first, second):
    return lax.optimization_barrier((first, second))


ORDER = ((0, 0), (1, 0), (2, 0), (3, 0), (3, 1), (1, 1), (2, 1), (0, 1), (3, 2), (1, 2), (3, 3), (1, 3), (2, 2), (2, 3), (0, 2), (0, 3))


def prepared(matrix, widths, groups):
    rows, columns = matrix.shape
    starts = [4 * sum(widths[:k]) for k in range(len(widths))]
    outs = [sum(widths[k] for k in group) for group in groups]
    width = widths[0]
    single = groups == [[0]] and width % 128 == 0
    if single:
        step = rows // 2 if rows % 32 == 0 else rows
        specs = [pl.BlockSpec((step, width), lambda r, d=d: (r, d)) for d in range(4)]
    else:
        step = 64 if rows % 64 == 0 else 32
        specs = [pl.BlockSpec((step, columns // 2), lambda r, d=d: (r, d)) for d in range(2)]

    def copy(sources, target, at, begin, size):
        for part in range(2):
            base = part * columns // 2
            low, high = max(begin, base), min(begin + size, base + columns // 2)
            if low < high:
                target[:, at + low - begin : at + high - begin] = sources[part][:, low - base : high - base].astype(BF)

    def kernel(*refs):
        sources, targets = refs[: len(specs)], refs[len(specs) :]
        for target, group in zip(targets, groups, strict=True):
            for d in range(4):
                if single:
                    target[d] = sources[d][...].astype(BF)
                    continue
                at = 0
                for k in group:
                    copy(sources, target.at[d], at, starts[k] + d * widths[k], widths[k])
                    at += widths[k]

    return pl.pallas_call(
        kernel,
        grid=(rows // step,),
        in_specs=specs,
        out_specs=[pl.BlockSpec((4, step, w), lambda r: (0, r, 0)) for w in outs],
        out_shape=[jax.ShapeDtypeStruct((4, rows, w), BF) for w in outs],
        compiler_params=pltpu.CompilerParams(vmem_limit_bytes=56 * 2**20),
        cost_estimate=pl.CostEstimate(flops=0, bytes_accessed=24 * rows * sum(outs), transcendentals=0),
    )(*[matrix] * len(specs))


def up_product(halves, matrix, start, width):
    count, features = halves[0].shape

    def kernel(first, second, matrix_ref, out):
        weights = matrix_ref[:, :, start : start + width].reshape(features, width)
        out[:count] = jnp.dot(first[...], weights, preferred_element_type=F32).astype(BF)
        out[count:] = jnp.dot(second[...], weights, preferred_element_type=F32).astype(BF)

    return pl.pallas_call(
        kernel,
        out_shape=jax.ShapeDtypeStruct((2 * count, width), BF),
        compiler_params=pltpu.CompilerParams(vmem_limit_bytes=8 * 2**20),
        cost_estimate=pl.CostEstimate(flops=0, bytes_accessed=1024, transcendentals=0),
    )(*halves, matrix)


def down_product(flag, pairs, matrix, places, before, split):
    n = len(pairs)
    features = matrix.shape[0] * matrix.shape[1]
    count = pairs[0][0].shape[0]
    half = count // 2

    def kernel(flag_ref, *refs):
        made, sent = refs[:n], refs[n : 2 * n]
        matrix_ref, rest = refs[2 * n], refs[2 * n + 1 :]
        for part in range(2):
            at = slice(part * half, part * half + half)
            total = rest[0][at, :] if before is not None else None
            for i, (start, width) in enumerate(places):
                hidden = jnp.where(flag_ref[0] == 1, made[i][at, :], sent[i][at, :width])
                weights = matrix_ref[:, :, start : start + width].reshape(features, width)
                term = lax.dot_general(hidden, weights, (((1,), (1,)), ((), ())), preferred_element_type=F32)
                total = term if total is None else total + term
            if not split:
                rest[-1][at, :] = total
            else:
                rest[part - 2][...] = total.astype(rest[part - 2].dtype)

    operands = [m for m, _ in pairs] + [t for _, t in pairs] + [matrix]
    if before is not None:
        operands.append(before)
    if split:
        shapes = [jax.ShapeDtypeStruct((half, features), F32), jax.ShapeDtypeStruct((half, features), BF)]
    else:
        shapes = [jax.ShapeDtypeStruct((count, features), F32)]
    depth = sum(w for _, w in places)
    return pl.pallas_call(
        kernel,
        in_specs=[pl.BlockSpec(memory_space=pltpu.SMEM)] + [pl.BlockSpec(memory_space=pltpu.VMEM)] * len(operands),
        out_shape=shapes,
        compiler_params=pltpu.CompilerParams(vmem_limit_bytes=16 * 2**20),
        cost_estimate=pl.CostEstimate(flops=0, bytes_accessed=1024, transcendentals=0),
    )(flag, *operands)


def planes(tokens, prompt_ids, modulation, trainer_up, trainer_down):
    me = lax.axis_index("mp")
    z = me // 4
    is_mid = (z == 1) | (z == 2)
    flag = is_mid.astype(jnp.int32).reshape(1)
    rows = trainer_up.shape[0]
    units = trainer_up.shape[1] // 4
    wide = units * 8 // 27 // 128 * 128
    widths = [wide, wide, wide, units - 3 * wide]
    down_t = trainer_down.T
    groups = [list(range(4 * p, 4 * p + 4)) for p in range(4)]

    def spread(sent, token=None):
        if token is not None:
            sent, token = tie(sent, token)
        return lax.all_to_all(sent, "mp", 0, 0, axis_index_groups=groups, tiled=True), token

    (up_first,) = prepared(trainer_up, widths, [[0]])
    up = [spread(up_first)[0]]
    xin = modulated(tokens, prompt_ids, modulation)
    owned = xin.shape[0]
    part = xin.shape[1] // 4

    def cut_in(m):
        return lax.dynamic_slice(xin, (0, (z ^ m) * part), (owned, part))

    received = [cut_in(0)] + [xor_mp(cut_in(m), 4 * m) for m in (1, 2, 3)]
    here = jnp.concatenate(in_order(received, z), axis=0)
    ready = list(prepared(trainer_up, widths, [[1], [2, 3]]))
    up[0], here = tie(up[0], here)
    ready[0], here = tie(ready[0], here)
    beside = xor_mp(here, 2)
    there = swap_rep(here)
    xs = [(here, xor_mp(here, 1)), None, None, None]

    to_other = [(i, i ^ 12) for i in range(16) if i // 4 in (1, 2)]
    early = [0, 0, 0, widths[2]]
    late = [0, widths[0], 0, widths[2]]
    outs = [None] * 4
    sums = [None] * 4
    left = [4] * 4
    held = [[] for _ in range(4)]
    pending = None
    down = []
    count = len(ORDER)
    mine, arrived, total, other, done = {}, {}, {}, {}, {}
    for s in range(count + 4):
        if s < count:
            block, k = ORDER[s]
            if s == 1:
                down_t, mine[0] = tie(down_t, mine[0])
                ready_down = list(prepared(down_t, widths, [[0, 1], [2, 3]]))
                beside, ready_down[0] = tie(beside, ready_down[0])
                beside, arrived[0], there, mine[0] = lax.optimization_barrier((beside, arrived[0], there, mine[0]))
                far = swap_rep(beside)
                xs[1] = (beside, xor_mp(beside, 1))
                total[0] = (mine[0].astype(F32) + arrived[0].astype(F32)).astype(BF)
                other[0] = lax.ppermute(total[0], "mp", to_other)
                xs[1] = (tie(xs[1][0], total[0])[0], xs[1][1])
                xs[2] = (there, xor_mp(there, 1))
            if s == 2:
                far, other[0] = tie(far, other[0])
                xs[3] = (far, xor_mp(far, 1))
            first, second = xs[block]
            if s >= 2:
                first, total[s - 2] = tie(first, total[s - 2])
            if s == 3:
                first, up[1] = tie(first, up[1])
            if s == 6:
                first, up[2] = tie(first, up[2])
            if s == 10:
                first, down[1] = tie(first, down[1])
            if pending is not None:
                first, outs[pending] = tie(first, outs[pending])
                pending = None
            mine[s] = up_product((first, second), up[min(k, 2)], early[k], widths[k])
        if s < count + 3:
            outgoing = []
            if s < count:
                outgoing.append(mine[s])
            if s >= 3:
                outgoing.append(done[s - 3])
            if len(outgoing) == 2:
                p, h = outgoing
                broad = max(p.shape[1], h.shape[1])
                p, h = [jnp.pad(v, ((0, 0), (0, broad - v.shape[1]))) for v in (p, h)]
                payload = jnp.where(is_mid, h, p)
            else:
                payload = outgoing[0]
            arrived[s] = xor_mp(payload, 4)
        if s < count:
            if s < 2:
                got, mine[s] = spread(ready[s], mine[s])
                up.append(got)
            if s in (2, 3):
                got, mine[s] = spread(ready_down[s - 2], mine[s])
                down.append(got)
            if s >= 2:
                arrived[s - 1], mine[s] = tie(arrived[s - 1], mine[s])
        if 0 <= s - 1 < count:
            if s >= 2:
                term = arrived[s - 1][:, : mine[s - 1].shape[1]]
                total[s - 1] = (mine[s - 1].astype(F32) + term.astype(F32)).astype(BF)
                other[s - 1] = lax.ppermute(total[s - 1], "mp", to_other)
            if s >= 2:
                other[s - 2], total[s - 1] = tie(other[s - 2], total[s - 1])
        if 0 <= s - 2 < count:
            summed = total[s - 2].astype(F32) + other[s - 2].astype(F32)
            done[s - 2] = jax.nn.gelu(summed, approximate=True).astype(BF)
        if 0 <= s - 4 < count:
            block, k = ORDER[s - 4]
            held[block].append((done[s - 4], arrived[s - 1], k))
            left[block] -= 1
            if len(held[block]) == 2:
                pairs = [(d, t) for d, t, _ in held[block]]
                places = [(late[i], widths[i]) for _, _, i in held[block]]
                held[block] = []
                last = left[block] == 0
                if last and block == 2:
                    from_3 = swap_rep(sums[3].astype(BF))
                    sent, from_3 = tie(pairs[1][1], from_3)
                    pairs[1] = (pairs[1][0], sent)
                if last and block == 0:
                    from_2 = swap_rep(sums[2].astype(BF))
                    from_1 = xor_mp((sums[1] + from_3.astype(F32)).astype(BF), 2)
                    sent, from_2, from_1 = lax.optimization_barrier((pairs[1][1], from_2, from_1))
                    pairs[1] = (pairs[1][0], sent)
                made = down_product(flag, pairs, down[int(last)], places, outs[block], last)
                if left[block] == 0:
                    sums[block] = made[0] + xor_mp(made[1], 1).astype(F32)
                else:
                    (outs[block],) = made
                    pending = block

    summed = (sums[0] + from_2.astype(F32) + from_1.astype(F32)).astype(BF)

    def cut_out(m):
        return lax.dynamic_slice(summed, ((z ^ m) * owned, 0), (owned, part))

    received = [cut_out(0)] + [xor_mp(cut_out(m), 4 * m) for m in (1, 2, 3)]
    mlp = jnp.concatenate(in_order(received, z), axis=1).astype(F32)
    prompt_ids, _ = tie(prompt_ids, mine[count - 1])
    gate = chosen(prompt_ids, modulation[0, :, 2:])[:, 0]
    return (tokens[0].astype(F32) + gate * mlp).astype(BF)[None]


def solution(mesh):
    in_specs = (
        P("rep", "mp", None),
        P("rep", "mp"),
        P("rep", None, None, None),
        P("mp", "rep"),
        P("rep", "mp"),
    )
    out_specs = P("rep", "mp", None)
    local = planes if (mesh.shape["rep"], mesh.shape["mp"]) == (2, 16) else gathered_weights
    return jax.shard_map(local, mesh=mesh, in_specs=in_specs, out_specs=out_specs, check_vma=False)
```

```python
import jax
import jax.numpy as jnp
from jax import lax
from jax.experimental import pallas as pl
from jax.experimental.pallas import tpu as pltpu
from jax.sharding import PartitionSpec as P

BF = jnp.bfloat16
F32 = jnp.float32


def chosen(prompt_ids, vectors):
    prompts_here = vectors.shape[0]
    onehot = (prompt_ids[0][:, None] == jnp.arange(prompts_here, dtype=jnp.int32)[None, :]).astype(F32)
    return jnp.einsum("tp,pkd->tkd", onehot, vectors, precision=lax.Precision.HIGHEST)


def modulated(tokens, prompt_ids, modulation):
    as_float = tokens[0].astype(F32)
    average = jnp.mean(as_float, axis=-1, keepdims=True)
    centred = as_float - average
    variance = jnp.mean(centred * centred, axis=-1, keepdims=True)
    normed = centred / jnp.sqrt(variance + 1e-06)
    vectors = chosen(prompt_ids, modulation[0, :, :2])
    return (normed * (1.0 + vectors[:, 1]) + vectors[:, 0]).astype(BF)


def gathered_weights(tokens, prompt_ids, modulation, trainer_up, trainer_down):
    xin = modulated(tokens, prompt_ids, modulation)
    gate = chosen(prompt_ids, modulation[0, :, 2:])[:, 0]
    up_rows = lax.all_gather(trainer_up.astype(BF), "rep", axis=1, tiled=True)
    w_up = lax.all_to_all(up_rows, "mp", split_axis=1, concat_axis=0, tiled=True)
    down_columns = lax.all_gather(trainer_down.astype(BF), "rep", axis=0, tiled=True)
    w_down = lax.all_to_all(down_columns, "mp", split_axis=0, concat_axis=1, tiled=True)
    everyone = lax.all_gather(xin, "mp", axis=0, tiled=True)
    hidden = jax.nn.gelu(jnp.dot(everyone, w_up, preferred_element_type=F32), approximate=True).astype(BF)
    partial = jnp.dot(hidden, w_down, preferred_element_type=F32).astype(BF)
    mlp = lax.psum_scatter(partial, "mp", scatter_dimension=0, tiled=True).astype(F32)
    return (tokens[0].astype(F32) + gate * mlp).astype(BF)[None]


def xor_mp(value, mask):
    return lax.ppermute(value, "mp", [(i, i ^ mask) for i in range(16)])


def swap_rep(value):
    return lax.ppermute(value, "rep", [(0, 1), (1, 0)])


def in_order(received, index):
    low = (index & 1) == 1
    high = (index & 2) == 2
    a, b, c, d = received
    a, b = jnp.where(low, b, a), jnp.where(low, a, b)
    c, d = jnp.where(low, d, c), jnp.where(low, c, d)
    return [jnp.where(high, c, a), jnp.where(high, d, b), jnp.where(high, a, c), jnp.where(high, b, d)]


def tie(first, second):
    return lax.optimization_barrier((first, second))


ORDER = ((0, 0), (1, 0), (2, 0), (3, 0), (3, 1), (1, 1), (2, 1), (0, 1), (3, 2), (1, 2), (3, 3), (1, 3), (2, 2), (2, 3), (0, 2), (0, 3))


def prepared(matrix, widths, groups):
    rows, columns = matrix.shape
    starts = [4 * sum(widths[:k]) for k in range(len(widths))]
    outs = [sum(widths[k] for k in group) for group in groups]
    width = widths[0]
    single = groups == [[0]] and width % 128 == 0
    if single:
        step = rows // 2 if rows % 32 == 0 else rows
        specs = [pl.BlockSpec((step, width), lambda r, d=d: (r, d)) for d in range(4)]
    else:
        step = 64 if rows % 64 == 0 else 32
        specs = [pl.BlockSpec((step, columns // 2), lambda r, d=d: (r, d)) for d in range(2)]

    def copy(sources, target, at, begin, size):
        for part in range(2):
            base = part * columns // 2
            low, high = max(begin, base), min(begin + size, base + columns // 2)
            if low < high:
                target[:, at + low - begin : at + high - begin] = sources[part][:, low - base : high - base].astype(BF)

    def kernel(*refs):
        sources, targets = refs[: len(specs)], refs[len(specs) :]
        for target, group in zip(targets, groups, strict=True):
            for d in range(4):
                if single:
                    target[d] = sources[d][...].astype(BF)
                    continue
                at = 0
                for k in group:
                    copy(sources, target.at[d], at, starts[k] + d * widths[k], widths[k])
                    at += widths[k]

    return pl.pallas_call(
        kernel,
        grid=(rows // step,),
        in_specs=specs,
        out_specs=[pl.BlockSpec((4, step, w), lambda r: (0, r, 0)) for w in outs],
        out_shape=[jax.ShapeDtypeStruct((4, rows, w), BF) for w in outs],
        compiler_params=pltpu.CompilerParams(vmem_limit_bytes=56 * 2**20),
        cost_estimate=pl.CostEstimate(flops=0, bytes_accessed=24 * rows * sum(outs), transcendentals=0),
    )(*[matrix] * len(specs))


def up_product(halves, matrix, start, width):
    count, features = halves[0].shape

    def kernel(first, second, matrix_ref, out):
        weights = matrix_ref[:, :, start : start + width].reshape(features, width)
        out[:count] = jnp.dot(first[...], weights, preferred_element_type=F32).astype(BF)
        out[count:] = jnp.dot(second[...], weights, preferred_element_type=F32).astype(BF)

    return pl.pallas_call(
        kernel,
        out_shape=jax.ShapeDtypeStruct((2 * count, width), BF),
        compiler_params=pltpu.CompilerParams(vmem_limit_bytes=8 * 2**20),
        cost_estimate=pl.CostEstimate(flops=0, bytes_accessed=1024, transcendentals=0),
    )(*halves, matrix)


def down_product(flag, pairs, matrix, places, before, split):
    n = len(pairs)
    features = matrix.shape[0] * matrix.shape[1]
    count = pairs[0][0].shape[0]
    half = count // 2

    def kernel(flag_ref, *refs):
        made, sent = refs[:n], refs[n : 2 * n]
        matrix_ref, rest = refs[2 * n], refs[2 * n + 1 :]
        for part in range(2):
            at = slice(part * half, part * half + half)
            total = rest[0][at, :] if before is not None else None
            for i, (start, width) in enumerate(places):
                hidden = jnp.where(flag_ref[0] == 1, made[i][at, :], sent[i][at, :width])
                weights = matrix_ref[:, :, start : start + width].reshape(features, width)
                term = lax.dot_general(hidden, weights, (((1,), (1,)), ((), ())), preferred_element_type=F32)
                total = term if total is None else total + term
            if not split:
                rest[-1][at, :] = total
            else:
                rest[part - 2][...] = total.astype(rest[part - 2].dtype)

    operands = [m for m, _ in pairs] + [t for _, t in pairs] + [matrix]
    if before is not None:
        operands.append(before)
    if split:
        shapes = [jax.ShapeDtypeStruct((half, features), F32), jax.ShapeDtypeStruct((half, features), BF)]
    else:
        shapes = [jax.ShapeDtypeStruct((count, features), F32)]
    depth = sum(w for _, w in places)
    return pl.pallas_call(
        kernel,
        in_specs=[pl.BlockSpec(memory_space=pltpu.SMEM)] + [pl.BlockSpec(memory_space=pltpu.VMEM)] * len(operands),
        out_shape=shapes,
        compiler_params=pltpu.CompilerParams(vmem_limit_bytes=16 * 2**20),
        cost_estimate=pl.CostEstimate(flops=0, bytes_accessed=1024, transcendentals=0),
    )(flag, *operands)


def planes(tokens, prompt_ids, modulation, trainer_up, trainer_down):
    me = lax.axis_index("mp")
    z = me // 4
    is_mid = (z == 1) | (z == 2)
    flag = is_mid.astype(jnp.int32).reshape(1)
    rows = trainer_up.shape[0]
    units = trainer_up.shape[1] // 4
    wide = units * 8 // 27 // 128 * 128
    widths = [wide, wide, wide, units - 3 * wide]
    down_t = trainer_down.T
    groups = [list(range(4 * p, 4 * p + 4)) for p in range(4)]

    def spread(sent, token=None):
        if token is not None:
            sent, token = tie(sent, token)
        return lax.all_to_all(sent, "mp", 0, 0, axis_index_groups=groups, tiled=True), token

    (up_first,) = prepared(trainer_up, widths, [[0]])
    up = [spread(up_first)[0]]
    xin = modulated(tokens, prompt_ids, modulation)
    owned = xin.shape[0]
    part = xin.shape[1] // 4

    def cut_in(m):
        return lax.dynamic_slice(xin, (0, (z ^ m) * part), (owned, part))

    received = [cut_in(0)] + [xor_mp(cut_in(m), 4 * m) for m in (1, 2, 3)]
    here = jnp.concatenate(in_order(received, z), axis=0)
    ready = list(prepared(trainer_up, widths, [[1], [2, 3]]))
    up[0], here = tie(up[0], here)
    ready[0], here = tie(ready[0], here)
    beside = xor_mp(here, 2)
    there = swap_rep(here)
    xs = [(here, xor_mp(here, 1)), None, None, None]

    to_other = [(i, i ^ 12) for i in range(16) if i // 4 in (1, 2)]
    early = [0, 0, 0, widths[2]]
    late = [0, widths[0], 0, widths[2]]
    outs = [None] * 4
    sums = [None] * 4
    left = [4] * 4
    held = [[] for _ in range(4)]
    pending = None
    down = []
    count = len(ORDER)
    mine, arrived, total, other, done = {}, {}, {}, {}, {}
    for s in range(count + 4):
        if s < count:
            block, k = ORDER[s]
            if s == 1:
                down_t, mine[0] = tie(down_t, mine[0])
                ready_down = list(prepared(down_t, widths, [[0, 1], [2, 3]]))
                beside, ready_down[0] = tie(beside, ready_down[0])
                beside, arrived[0], there, mine[0] = lax.optimization_barrier((beside, arrived[0], there, mine[0]))
                far = swap_rep(beside)
                xs[1] = (beside, xor_mp(beside, 1))
                total[0] = (mine[0].astype(F32) + arrived[0].astype(F32)).astype(BF)
                other[0] = lax.ppermute(total[0], "mp", to_other)
                xs[1] = (tie(xs[1][0], total[0])[0], xs[1][1])
                xs[2] = (there, xor_mp(there, 1))
            if s == 2:
                far, other[0] = tie(far, other[0])
                xs[3] = (far, xor_mp(far, 1))
            first, second = xs[block]
            if s >= 2:
                first, total[s - 2] = tie(first, total[s - 2])
            if s == 3:
                first, up[1] = tie(first, up[1])
            if s == 5:
                first, up[2] = tie(first, up[2])
            if s == 11:
                first, down[1] = tie(first, down[1])
            if pending is not None:
                first, outs[pending] = tie(first, outs[pending])
                pending = None
            mine[s] = up_product((first, second), up[min(k, 2)], early[k], widths[k])
        if s < count + 3:
            outgoing = []
            if s < count:
                outgoing.append(mine[s])
            if s >= 3:
                outgoing.append(done[s - 3])
            if len(outgoing) == 2:
                p, h = outgoing
                broad = max(p.shape[1], h.shape[1])
                p, h = [jnp.pad(v, ((0, 0), (0, broad - v.shape[1]))) for v in (p, h)]
                payload = jnp.where(is_mid, h, p)
            else:
                payload = outgoing[0]
            arrived[s] = xor_mp(payload, 4)
        if s < count:
            if s < 2:
                got, mine[s] = spread(ready[s], mine[s])
                up.append(got)
            if s in (2, 3):
                got, mine[s] = spread(ready_down[s - 2], mine[s])
                down.append(got)
            if s >= 2:
                arrived[s - 1], mine[s] = tie(arrived[s - 1], mine[s])
        if 0 <= s - 1 < count:
            if s >= 2:
                term = arrived[s - 1][:, : mine[s - 1].shape[1]]
                total[s - 1] = (mine[s - 1].astype(F32) + term.astype(F32)).astype(BF)
                other[s - 1] = lax.ppermute(total[s - 1], "mp", to_other)
            if s >= 2:
                other[s - 2], total[s - 1] = tie(other[s - 2], total[s - 1])
        if 0 <= s - 2 < count:
            summed = total[s - 2].astype(F32) + other[s - 2].astype(F32)
            done[s - 2] = jax.nn.gelu(summed, approximate=True).astype(BF)
        if 0 <= s - 4 < count:
            block, k = ORDER[s - 4]
            held[block].append((done[s - 4], arrived[s - 1], k))
            left[block] -= 1
            if len(held[block]) == 2:
                pairs = [(d, t) for d, t, _ in held[block]]
                places = [(late[i], widths[i]) for _, _, i in held[block]]
                held[block] = []
                last = left[block] == 0
                if last and block == 2:
                    from_3 = swap_rep(sums[3].astype(BF))
                    sent, from_3 = tie(pairs[1][1], from_3)
                    pairs[1] = (pairs[1][0], sent)
                if last and block == 0:
                    from_2 = swap_rep(sums[2].astype(BF))
                    from_1 = xor_mp((sums[1] + from_3.astype(F32)).astype(BF), 2)
                    sent, from_2, from_1 = lax.optimization_barrier((pairs[1][1], from_2, from_1))
                    pairs[1] = (pairs[1][0], sent)
                made = down_product(flag, pairs, down[int(last)], places, outs[block], last)
                if left[block] == 0:
                    sums[block] = made[0] + xor_mp(made[1], 1).astype(F32)
                else:
                    (outs[block],) = made
                    pending = block

    summed = (sums[0] + from_2.astype(F32) + from_1.astype(F32)).astype(BF)

    def cut_out(m):
        return lax.dynamic_slice(summed, ((z ^ m) * owned, 0), (owned, part))

    received = [cut_out(0)] + [xor_mp(cut_out(m), 4 * m) for m in (1, 2, 3)]
    mlp = jnp.concatenate(in_order(received, z), axis=1).astype(F32)
    prompt_ids, _ = tie(prompt_ids, mine[count - 1])
    gate = chosen(prompt_ids, modulation[0, :, 2:])[:, 0]
    return (tokens[0].astype(F32) + gate * mlp).astype(BF)[None]


def solution(mesh):
    in_specs = (
        P("rep", "mp", None),
        P("rep", "mp"),
        P("rep", None, None, None),
        P("mp", "rep"),
        P("rep", "mp"),
    )
    out_specs = P("rep", "mp", None)
    local = planes if (mesh.shape["rep"], mesh.shape["mp"]) == (2, 16) else gathered_weights
    return jax.shard_map(local, mesh=mesh, in_specs=in_specs, out_specs=out_specs, check_vma=False)
```
